32 devices in a mesh: groups: 2 (over x), orb: 16 (over z, y, core).
Axes of the slice: x: 2, y: 2, z: 4, core: 2. Of those that a mesh axis runs over, the one named last changes fastest.
Arguments:
- blocks: bfloat16 [192, 1536, 384], P(('groups', 'orb')), parts along dimension 0, may hold values from -1 to 1
- pao_energy: float32 [192, 384], P(('groups', 'orb')), parts along dimension 0, may hold values from 0.5 to 3
- occ_energy: float32 [192], P(('groups', 'orb')), parts along dimension 0, may hold values from -1.5 to -0.3
- dom_blocks: int32 [192], P(('groups', 'orb')), parts along dimension 0, may hold values from 1 to 3
- pairs: int32 [512, 2], P(('groups', 'orb')), parts along dimension 0, may hold values from -1 to 95, as said below
Outputs:
- pair_energy: float32 [512], P(('groups', 'orb')), parts along dimension 0
- density: float32 [192, 384, 384], P(('groups', 'orb')), parts along dimension 0
The draws below stay inside these ranges and needn't reach their ends.
There are 2 independent parts, one for each index of `groups`. The reference program is written for one: setup_inputs(seed, part) draws one part's arguments, and reference() takes and returns one part's arrays. A program takes and returns all parts, laid end to end along the dimension named above; each array names one. Nothing has to cross between parts.
Inputs may be any that keep to these rules, and one draw needn't show every extreme that they name: `pairs`: the slots of device d are rows d * 16 to (d + 1) * 16 - 1; the live ones come first, their first orbital is owned by d (one of orbitals d * 6 to (d + 1) * 6 - 1) and their second orbital is a different orbital owned by d - 1, d or d + 1. A device has 1 to 16 live slots; in every draw some device has all 16 live and some device only one. Empty slots hold -1 twice.
All inputs are finite; a program needn't handle non-finite values.
Results may differ from the reference program's by a relative error of at most 0.0021.
Values may be sent and summed in bfloat16 or wider, within the bound.
A program may use at most 128 MiB of HBM per device.

```python
import math
import jax
import jax.numpy as jnp
from jax import lax

AUX = 1536
DOM = 384
GRAIN = 128
ORB_DEV = 6
PAIR_DEV = 16
NORB = 96
NPAIR = 256
N_ORB = 16


def draw_pairs(key, part):
    key = jax.random.fold_in(key, 11)
    keys = jax.random.split(key, 5)
    index = jnp.arange(NPAIR, dtype=jnp.int32)
    owner = index // PAIR_DEV
    slot = index % PAIR_DEV
    counts = jax.random.randint(keys[0], (N_ORB,), 1, PAIR_DEV + 1)
    fullest = jax.random.randint(keys[1], (), 0, N_ORB)
    devices = jnp.arange(N_ORB, dtype=jnp.int32)
    counts = jnp.where(devices == fullest, PAIR_DEV, counts)
    counts = jnp.where(devices == (fullest + 1) % N_ORB, 1, counts)
    live = slot < counts[owner]
    first_local = jax.random.randint(keys[2], (NPAIR,), 0, ORB_DEV)
    first_local = jnp.where(index == (N_ORB - 1) * PAIR_DEV, ORB_DEV - 1, first_local)
    offset = jax.random.randint(keys[3], (NPAIR,), -1, 2)
    partner = jnp.clip(owner + offset, 0, N_ORB - 1)
    second_local = jax.random.randint(keys[4], (NPAIR,), 0, ORB_DEV)
    clash = (partner == owner) & (second_local == first_local)
    second_local = jnp.where(clash, (first_local + 1) % ORB_DEV, second_local)
    first = owner * ORB_DEV + first_local
    second = partner * ORB_DEV + second_local
    empty = jnp.full((NPAIR,), -1, jnp.int32)
    return jnp.stack([jnp.where(live, first, empty), jnp.where(live, second, empty)], 1).astype(jnp.int32)


def place_ends(values, own_key, low, high):
    place = [jax.random.randint(jax.random.fold_in(own_key, axis), (), 0, length) for axis, length in enumerate(values.shape)]
    widest = values.shape.index(max(values.shape))
    neighbour = place[:widest] + [(place[widest] + 1) % values.shape[widest]] + place[widest + 1:]
    return values.at[tuple(place)].set(low).at[tuple(neighbour)].set(high)


def levels(key, shape, cuts, smallest, largest):
    loudness, own = 1.0, jax.random.fold_in(key, 6)
    for position, shards_of in cuts:
        draws = jnp.exp(jax.random.uniform(jax.random.fold_in(own, position), (shards_of,), jnp.float32, smallest / len(cuts), largest / len(cuts)))
        loudness = loudness * jnp.repeat(draws, shape[position] // shards_of).reshape([-1 if axis == position else 1 for axis in range(len(shape))])
    return loudness


def gaussian(own_key, shape, scale, limit, pieces=(), kind=jnp.bfloat16):
    entries = scale * jax.random.normal(own_key, shape, jnp.float32)
    if pieces:
        entries = entries * levels(own_key, shape, pieces, -0.22, 0.18)
    return jnp.clip(entries, -limit, limit).astype(kind)


def setup_inputs(seed: int = 0, part: int = 0) -> dict:
    seeds = jax.random.split(jax.random.key(seed), 6)
    part_splits = jax.random.split(jax.random.fold_in(seeds[5], part), 6)
    blocks = gaussian(part_splits[0], (NORB, AUX, DOM), 0.16, 1.0, ((0, 16),))
    pao_energy = jnp.clip(0.5 + 2.5 * jax.random.uniform(part_splits[1], (NORB, DOM), jnp.float32) ** levels(part_splits[1], (NORB, DOM), ((0, 16),), -0.2, 0.2), 0.5, 3.0)
    occ_energy = jnp.clip(-1.5 + 1.2 * jax.random.uniform(part_splits[2], (NORB,), jnp.float32) ** levels(part_splits[2], (NORB,), ((0, 16),), -0.2, 0.2), -1.5, -0.3)
    dom_blocks = place_ends(jax.random.randint(part_splits[3], (NORB,), 1, DOM // GRAIN + 1), jax.random.fold_in(part_splits[3], 1), 1, (DOM // GRAIN + 1) - 1).astype(jnp.int32)
    pairs = draw_pairs(jax.random.fold_in(jax.random.fold_in(seeds[5], part), 71), part)
    return dict(blocks=blocks, pao_energy=pao_energy, occ_energy=occ_energy, dom_blocks=dom_blocks, pairs=pairs)


def reference(blocks, pao_energy, occ_energy, dom_blocks, pairs):
    column = jnp.arange(DOM, dtype=jnp.int32)
    live_cols = column[None, :] < (dom_blocks * GRAIN)[:, None]
    shifted = pao_energy - occ_energy[:, None]
    factor = 1.0 / math.sqrt(DOM)

    def pair_step(density, pair):
        first = jnp.maximum(pair[0], 0)
        second = jnp.maximum(pair[1], 0)
        live = pair[0] >= 0
        left_block = jnp.where(live_cols[first][None, :], blocks[first], jnp.zeros((), blocks.dtype)).astype(jnp.bfloat16)
        right_block = jnp.where(live_cols[second][None, :], blocks[second], jnp.zeros((), blocks.dtype)).astype(jnp.bfloat16)
        exchange = lax.dot_general(left_block, right_block, (((0,), (0,)), ((), ())), preferred_element_type=jnp.float32)
        denom = shifted[first][:, None] + shifted[second][None, :]
        amplitude = jnp.where(live, -exchange / denom, jnp.zeros((), jnp.float32))
        energy = 2.0 * jnp.sum(exchange * amplitude)
        rounded = amplitude.astype(jnp.bfloat16)
        first_part = jnp.dot(rounded, rounded.T, preferred_element_type=jnp.float32) * factor
        second_part = lax.dot_general(rounded, rounded, (((0,), (0,)), ((), ())), preferred_element_type=jnp.float32) * factor
        density = density.at[first].add(first_part)
        density = density.at[second].add(second_part)
        return (density, energy)
    start = jnp.zeros((NORB, DOM, DOM), jnp.float32)
    density, energies = lax.scan(pair_step, start, pairs)
    return (energies, density)
```

```python
import functools
import math

import jax
import jax.numpy as jnp
from jax import lax
from jax.experimental import pallas as pl
from jax.experimental.pallas import tpu as pltpu
from jax.sharding import PartitionSpec as P

GRAIN = 128
MESH = pl.DeviceIdType.MESH
NT = (((1,), (1,)), ((), ()))
TN = (((0,), (0,)), ((), ()))
WINDOW = 6


def kernel(
    size, n, aux, width, factor,
    blocks, info, wself, wleft,
    dens, eself, eleft, eright,
    own, got, left_t, linfo, own_col, left_col, acc, ret_out, ret_in, ein,
    own_sem, blk_send, blk_recv, info_sem, ret_send, ret_recv, e_send, e_recv,
):
    me = lax.axis_index("orb")
    has_left = me > 0
    has_right = me < size - 1
    right = jnp.minimum(me + 1, size - 1)
    left = jnp.maximum(me - 1, 0)
    reach = n // 2

    barrier = pltpu.get_barrier_semaphore()

    @pl.when(has_left)
    def _():
        pl.semaphore_signal(barrier, inc=1, device_id={"orb": left}, device_id_type=MESH)

    @pl.when(has_right)
    def _():
        pl.semaphore_signal(barrier, inc=1, device_id={"orb": right}, device_id_type=MESH)

    def own_copy(k):
        return pltpu.make_async_copy(blocks.at[k], own.at[k], own_sem.at[k])

    def blk_copy(k):
        return pltpu.make_async_remote_copy(
            src_ref=blocks.at[k], dst_ref=got.at[k], send_sem=blk_send.at[k], recv_sem=blk_recv.at[k],
            device_id={"orb": right}, device_id_type=MESH,
        )

    def info_copy():
        return pltpu.make_async_remote_copy(
            src_ref=info, dst_ref=linfo, send_sem=info_sem.at[0], recv_sem=info_sem.at[1],
            device_id={"orb": right}, device_id_type=MESH,
        )

    def ret_copy(k):
        return pltpu.make_async_remote_copy(
            src_ref=ret_out.at[k], dst_ref=ret_in.at[k], send_sem=ret_send.at[k], recv_sem=ret_recv.at[k],
            device_id={"orb": left}, device_id_type=MESH,
        )

    def e_copy(k):
        return pltpu.make_async_remote_copy(
            src_ref=eleft.at[pl.ds(k * n, n)], dst_ref=ein.at[pl.ds(k * n, n)],
            send_sem=e_send.at[k], recv_sem=e_recv.at[k],
            device_id={"orb": left}, device_id_type=MESH,
        )

    for k in range(n):
        own_copy(k).start()

    peers = has_left.astype(jnp.int32) + has_right.astype(jnp.int32)
    pl.semaphore_wait(barrier, peers)

    @pl.when(has_right)
    def _():
        info_copy().start()
        for k in range(min(WINDOW, n)):
            blk_copy(k).start()

    def columns(source, target):
        turned = jnp.transpose(source[0:8, :])
        for k in range(n):
            target[k] = jnp.broadcast_to(turned[:, k : k + 1], (width, GRAIN))

    columns(info, own_col)
    dens[...] = jnp.zeros_like(dens)

    @pl.loop(0, n)
    def _(k):
        own_copy(k).wait()
        own[k] = own[k] * info[pl.ds(8 + k, 1), :].astype(jnp.bfloat16)

    def product(col, r, w):
        exchange = jnp.dot(left_t[...], own[r], preferred_element_type=jnp.float32)
        denom = jnp.concatenate([col] * (width // GRAIN), axis=1) + info[pl.ds(r, 1), :]
        amplitude = -exchange / denom
        parts = jnp.sum((exchange * amplitude).reshape(width // 8, 8, width), axis=0)
        energy = parts[:, :GRAIN]
        for c in range(1, width // GRAIN):
            energy = energy + parts[:, c * GRAIN : (c + 1) * GRAIN]
        rounded = amplitude.astype(jnp.bfloat16)
        first = lax.dot_general(rounded, rounded, NT, preferred_element_type=jnp.float32)
        second = lax.dot_general(rounded, rounded, TN, preferred_element_type=jnp.float32)
        scale = w * factor
        dens[r] += second * scale
        return energy, first * scale

    @pl.loop(0, n)
    def _(i):
        left_t[...] = jnp.transpose(own[i])
        total = None
        for t in range(1, reach + 1):
            at = i * reach + (t - 1)
            energy, first = product(own_col[i], lax.rem(i + t, n), wself[pl.ds(at, 1), :])
            eself[at] = energy
            total = first if total is None else total + first
        dens[i] += total

    @pl.when(has_left)
    def _():
        info_copy().wait_recv()
        columns(linfo, left_col)

    step = 2 if n % 2 == 0 else 1

    @pl.loop(0, n)
    def _(k):
        @pl.when(has_left)
        def _():
            blk_copy(k).wait_recv()
            left_t[...] = jnp.transpose(got[k] * linfo[pl.ds(8 + k, 1), :].astype(jnp.bfloat16))
            acc[...] = jnp.zeros_like(acc)

            @pl.loop(0, n // step)
            def _(q):
                total = None
                for s in range(step):
                    r = q * step + s
                    at = k * n + r
                    w = linfo[pl.ds(16 + at, 1), :] + wleft[pl.ds(at, 1), :]
                    energy, first = product(left_col[k], r, w)
                    eleft[at] = energy
                    total = first if total is None else total + first
                acc[...] += total

            ret_out[k] = acc[...].astype(jnp.bfloat16)
            ret_copy(k).start()
            e_copy(k).start()

        if WINDOW < n:
            @pl.when(has_right & (k + WINDOW < n))
            def _():
                blk_copy(k).wait_send()
                blk_copy(k + WINDOW).start()

    @pl.when(has_right)
    def _():
        info_copy().wait_send()

        @pl.loop(max(n - WINDOW, 0), n)
        def _(k):
            blk_copy(k).wait_send()

        @pl.loop(0, n)
        def _(k):
            ret_copy(k).wait_recv()
            dens[k] += ret_in[k].astype(jnp.float32)
            e_copy(k).wait_recv()

        eright[...] = ein[...]

    @pl.when(has_left)
    def _():
        @pl.loop(0, n)
        def _(k):
            ret_copy(k).wait_send()
            e_copy(k).wait_send()

    @pl.when(jnp.logical_not(has_right))
    def _():
        eright[...] = jnp.zeros_like(eright)

    @pl.when(jnp.logical_not(has_left))
    def _():
        eleft[...] = jnp.zeros_like(eleft)


def per_device(blocks, pao_energy, occ_energy, dom_blocks, pairs):
    n, aux, width = blocks.shape
    size = lax.axis_size("orb")
    reach = n // 2
    factor = 1.0 / math.sqrt(width)
    start = lax.axis_index("orb") * n
    column = lax.broadcasted_iota(jnp.int32, (n, width), 1)
    live_cols = (column < (dom_blocks * GRAIN)[:, None]).astype(jnp.float32)
    shifted = pao_energy - occ_energy[:, None]

    live = pairs[:, 0] >= 0
    i = pairs[:, 0] - start
    j = pairs[:, 1] - start
    side = jnp.where(j < 0, 0, jnp.where(j >= n, 2, 1))
    ahead = jnp.mod(j - i, n)
    near = (ahead < n - ahead) | ((2 * ahead == n) & (i < j))
    self_at = jnp.where(near, i * reach + ahead - 1, j * reach + (n - ahead) - 1)
    n_self = n * reach
    at = jnp.where(
        side == 1, self_at,
        jnp.where(side == 0, n_self + (j + n) * n + i, n_self + n * n + i * n + (j - n)),
    )
    hot = ((at[:, None] == jnp.arange(n_self + 2 * n * n)[None, :]) & live[:, None]).astype(jnp.float32)
    weight = jnp.broadcast_to(jnp.sum(hot, axis=0)[:, None], (hot.shape[1], width))
    pad = jnp.zeros((8 - n, width), jnp.float32)
    info = jnp.concatenate([shifted, pad, live_cols, pad, weight[n_self + n * n :]], axis=0)
    wself = weight[:n_self]
    wleft = weight[n_self : n_self + n * n]

    f32, bf16 = jnp.float32, jnp.bfloat16
    vmem = pl.BlockSpec(memory_space=pltpu.VMEM)
    dens, eself, eleft, eright = pl.pallas_call(
        functools.partial(kernel, size, n, aux, width, factor),
        out_shape=(
            jax.ShapeDtypeStruct((n, width, width), f32),
            jax.ShapeDtypeStruct((n_self, 8, GRAIN), f32),
            jax.ShapeDtypeStruct((n * n, 8, GRAIN), f32),
            jax.ShapeDtypeStruct((n * n, 8, GRAIN), f32),
        ),
        in_specs=[pl.BlockSpec(memory_space=pl.ANY), vmem, vmem, vmem],
        out_specs=(vmem, vmem, vmem, vmem),
        scratch_shapes=[
            pltpu.VMEM((n, aux, width), bf16),
            pltpu.VMEM((n, aux, width), bf16),
            pltpu.VMEM((width, aux), bf16),
            pltpu.VMEM(info.shape, f32),
            pltpu.VMEM((n, width, GRAIN), f32),
            pltpu.VMEM((n, width, GRAIN), f32),
            pltpu.VMEM((width, width), f32),
            pltpu.VMEM((n, width, width), bf16),
            pltpu.VMEM((n, width, width), bf16),
            pltpu.VMEM((n * n, 8, GRAIN), f32),
            pltpu.SemaphoreType.DMA((n,)),
            pltpu.SemaphoreType.DMA((n,)),
            pltpu.SemaphoreType.DMA((n,)),
            pltpu.SemaphoreType.DMA((2,)),
            pltpu.SemaphoreType.DMA((n,)),
            pltpu.SemaphoreType.DMA((n,)),
            pltpu.SemaphoreType.DMA((n,)),
            pltpu.SemaphoreType.DMA((n,)),
        ],
        compiler_params=pltpu.CompilerParams(
            collective_id=0, has_side_effects=True, vmem_limit_bytes=52 * 1024 * 1024
        ),
    )(blocks, info, wself, wleft)

    table = jnp.concatenate([jnp.sum(e, axis=(1, 2)) for e in (eself, eleft, eright)])
    energies = 2.0 * jnp.sum(jnp.where(hot > 0, table[None, :], 0.0), axis=1)
    return (energies, dens)


def solution(mesh):
    in_specs = (
        P(("groups", "orb"), None, None),
        P(("groups", "orb"), None),
        P(("groups", "orb")),
        P(("groups", "orb")),
        P(("groups", "orb"), None),
    )
    out_specs = (P(("groups", "orb")), P(("groups", "orb"), None, None))
    return jax.shard_map(
        per_device, mesh=mesh, in_specs=in_specs, out_specs=out_specs, check_vma=False
    )
```

```python
import functools
import math

import jax
import jax.numpy as jnp
from jax import lax
from jax.experimental import pallas as pl
from jax.experimental.pallas import tpu as pltpu
from jax.sharding import PartitionSpec as P

GRAIN = 128
MESH = pl.DeviceIdType.MESH
NT = (((1,), (1,)), ((), ()))
TN = (((0,), (0,)), ((), ()))


def kernel(
    size, factor,
    blocks, pao, occ, dom, pairs,
    dens, energies,
    own, got, left_t, info, linfo, wtab, wright, own_col, left_col, acc, ret_out, ret_in, etab, ein,
    own_sem, blk_send, blk_recv, info_sem, w_sem, ret_send, ret_recv, e_sem,
):
    n, _, width = blocks.shape
    tiles = width // GRAIN
    reach = n // 2
    edge = wright.shape[0]
    at_left, at_self = edge, 2 * edge
    me = lax.axis_index("orb")
    has_left = me > 0
    has_right = me < size - 1
    right = jnp.minimum(me + 1, size - 1)
    left = jnp.maximum(me - 1, 0)

    barrier = pltpu.get_barrier_semaphore()

    @pl.when(has_left)
    def _():
        pl.semaphore_signal(barrier, inc=1, device_id={"orb": left}, device_id_type=MESH)

    @pl.when(has_right)
    def _():
        pl.semaphore_signal(barrier, inc=1, device_id={"orb": right}, device_id_type=MESH)

    def own_copy(k):
        return pltpu.make_async_copy(blocks.at[k], own.at[k], own_sem.at[k])

    def to_right(source, target, send_sem, recv_sem):
        return pltpu.make_async_remote_copy(
            src_ref=source, dst_ref=target, send_sem=send_sem, recv_sem=recv_sem,
            device_id={"orb": right}, device_id_type=MESH,
        )

    def to_left(source, target, send_sem, recv_sem):
        return pltpu.make_async_remote_copy(
            src_ref=source, dst_ref=target, send_sem=send_sem, recv_sem=recv_sem,
            device_id={"orb": left}, device_id_type=MESH,
        )

    def blk_copy(k):
        return to_right(blocks.at[k], got.at[k], blk_send.at[k], blk_recv.at[k])

    def info_copy():
        return to_right(info, linfo, info_sem.at[0], info_sem.at[1])

    def w_copy():
        return to_right(wtab.at[pl.ds(0, edge)], wright, w_sem.at[0], w_sem.at[1])

    def ret_copy(k):
        return to_left(ret_out.at[k], ret_in.at[k], ret_send.at[k], ret_recv.at[k])

    def e_copy():
        return to_left(etab.at[pl.ds(at_left, edge)], ein, e_sem.at[0], e_sem.at[1])

    for k in range(n):
        own_copy(k).start()

    info[...] = jnp.zeros_like(info)
    column = lax.broadcasted_iota(jnp.int32, (1, width), 1)
    for k in range(n):
        info[k : k + 1, :] = pao[k : k + 1, :] - occ[k]
        info[8 + k : 9 + k, :] = jnp.where(column < dom[k] * GRAIN, 1.0, 0.0)

    start = me * n
    live = pairs[:, 0:1] >= 0
    i = pairs[:, 0:1] - start
    j = pairs[:, 1:2] - start
    ahead = jnp.where(j < i, j - i + n, j - i)
    near = (ahead < n - ahead) | ((2 * ahead == n) & (i < j))
    place = at_self + jnp.where(near, i * reach + ahead - 1, j * reach + (n - ahead) - 1)
    place = jnp.where(j < 0, at_left + (j + n) * n + i, place)
    place = jnp.where(j >= n, i * n + (j - n), place)
    place = jnp.where(live, place, -1)
    spots = lax.broadcasted_iota(jnp.int32, (pairs.shape[0], GRAIN), 1)
    hot = jnp.where(place == spots, 1.0, 0.0)
    counts = jnp.sum(hot, axis=0, keepdims=True)
    wtab[...] = jnp.transpose(jnp.broadcast_to(counts, (GRAIN, GRAIN)))

    peers = has_left.astype(jnp.int32) + has_right.astype(jnp.int32)
    pl.semaphore_wait(barrier, peers)

    @pl.when(has_right)
    def _():
        info_copy().start()
        w_copy().start()
        for k in range(n):
            blk_copy(k).start()

    def columns(source, target):
        turned = jnp.transpose(source[0:8, :])
        for k in range(n):
            target[k] = jnp.broadcast_to(turned[:, k : k + 1], (width, GRAIN))

    def wide(x):
        return jnp.concatenate([x] * tiles, axis=1)

    columns(info, own_col)
    dens[...] = jnp.zeros_like(dens)
    etab[...] = jnp.zeros_like(etab)

    @pl.loop(0, n)
    def _(k):
        own_copy(k).wait()
        own[k] = own[k] * info[pl.ds(8 + k, 1), :].astype(jnp.bfloat16)

    def product(col, r, w, spot):
        exchange = jnp.dot(left_t[...], own[r], preferred_element_type=jnp.float32)
        denom = wide(col) + info[pl.ds(r, 1), :]
        amplitude = -exchange / denom
        parts = jnp.sum((exchange * amplitude).reshape(width // 8, 8, width), axis=0)
        energy = parts[:, :GRAIN]
        for c in range(1, tiles):
            energy = energy + parts[:, c * GRAIN : (c + 1) * GRAIN]
        etab[pl.ds(spot, 1), :] = jnp.sum(energy, axis=0, keepdims=True)
        rounded = amplitude.astype(jnp.bfloat16)
        first = lax.dot_general(rounded, rounded, NT, preferred_element_type=jnp.float32)
        second = lax.dot_general(rounded, rounded, TN, preferred_element_type=jnp.float32)
        scale = wide(w) * factor
        dens[r] += second * scale
        return first * scale

    @pl.loop(0, n)
    def _(i):
        left_t[...] = jnp.transpose(own[i])
        total = None
        for t in range(1, reach + 1):
            spot = at_self + i * reach + (t - 1)
            first = product(own_col[i], lax.rem(i + t, n), wtab[pl.ds(spot, 1), :], spot)
            total = first if total is None else total + first
        dens[i] += total

    upper = [(a, b) for a in range(tiles) for b in range(a, tiles)]
    step = 2 if n % 2 == 0 else 1

    @pl.when(has_left)
    def _():
        info_copy().wait_recv()
        w_copy().wait_recv()
        columns(linfo, left_col)

        @pl.loop(0, n)
        def _(k):
            blk_copy(k).wait_recv()

            @pl.when(k == n - 1)
            def _():
                @pl.loop(0, n - 1)
                def _(m):
                    ret_copy(m).start()

            left_t[...] = jnp.transpose(got[k] * linfo[pl.ds(8 + k, 1), :].astype(jnp.bfloat16))
            acc[...] = jnp.zeros_like(acc)

            @pl.loop(0, n // step)
            def _(q):
                total = None
                for s in range(step):
                    r = q * step + s
                    at = k * n + r
                    w = wright[pl.ds(at, 1), :] + wtab[pl.ds(at_left + at, 1), :]
                    first = product(left_col[k], r, w, at_left + at)
                    total = first if total is None else total + first
                acc[...] += total

            for u, (a, b) in enumerate(upper):
                ret_out[k, u] = acc[a * GRAIN : (a + 1) * GRAIN, b * GRAIN : (b + 1) * GRAIN].astype(jnp.bfloat16)

        ret_copy(n - 1).start()
        e_copy().start()

    @pl.when(has_right)
    def _():
        info_copy().wait_send()
        w_copy().wait_send()

        @pl.loop(0, n)
        def _(k):
            blk_copy(k).wait_send()

        @pl.loop(0, n)
        def _(k):
            ret_copy(k).wait_recv()
            for u, (a, b) in enumerate(upper):
                rows, cols = pl.ds(a * GRAIN, GRAIN), pl.ds(b * GRAIN, GRAIN)
                term = ret_in[k, u].astype(jnp.float32)
                dens[k, rows, cols] += term
                if a != b:
                    dens[k, cols, rows] += jnp.transpose(term)

        e_copy().wait_recv()
        etab[0:edge, :] = ein[...]

    table = jnp.sum(jnp.transpose(etab[...]), axis=0, keepdims=True)
    energies[...] = 2.0 * jnp.sum(hot * table, axis=1, keepdims=True)

    @pl.when(has_left)
    def _():
        e_copy().wait_send()

        @pl.loop(0, n)
        def _(k):
            ret_copy(k).wait_send()


def per_device(blocks, pao_energy, occ_energy, dom_blocks, pairs):
    n, aux, width = blocks.shape
    size = lax.axis_size("orb")
    factor = 1.0 / math.sqrt(width)
    edge = -(-n * n // 8) * 8
    tiles = width // GRAIN
    upper = tiles * (tiles + 1) // 2
    f32, bf16 = jnp.float32, jnp.bfloat16
    vmem = pl.BlockSpec(memory_space=pltpu.VMEM)
    smem = pl.BlockSpec(memory_space=pltpu.SMEM)
    many = pltpu.SemaphoreType.DMA((n,))
    two = pltpu.SemaphoreType.DMA((2,))
    dens, energies = pl.pallas_call(
        functools.partial(kernel, size, factor),
        out_shape=(
            jax.ShapeDtypeStruct((n, width, width), f32),
            jax.ShapeDtypeStruct((pairs.shape[0], 1), f32),
        ),
        in_specs=[pl.BlockSpec(memory_space=pl.ANY), vmem, smem, smem, vmem],
        out_specs=(vmem, vmem),
        scratch_shapes=[
            pltpu.VMEM((n, aux, width), bf16),
            pltpu.VMEM((n, aux, width), bf16),
            pltpu.VMEM((width, aux), bf16),
            pltpu.VMEM((16, width), f32),
            pltpu.VMEM((16, width), f32),
            pltpu.VMEM((GRAIN, GRAIN), f32),
            pltpu.VMEM((edge, GRAIN), f32),
            pltpu.VMEM((n, width, GRAIN), f32),
            pltpu.VMEM((n, width, GRAIN), f32),
            pltpu.VMEM((width, width), f32),
            pltpu.VMEM((n, upper, GRAIN, GRAIN), bf16),
            pltpu.VMEM((n, upper, GRAIN, GRAIN), bf16),
            pltpu.VMEM((GRAIN, GRAIN), f32),
            pltpu.VMEM((edge, GRAIN), f32),
            many, many, many, two, two, many, many, two,
        ],
        compiler_params=pltpu.CompilerParams(
            collective_id=0, has_side_effects=True, vmem_limit_bytes=52 * 1024 * 1024
        ),
    )(blocks, pao_energy, occ_energy, dom_blocks, pairs)
    return (energies[:, 0], dens)


def solution(mesh):
    in_specs = (
        P(("groups", "orb"), None, None),
        P(("groups", "orb"), None),
        P(("groups", "orb")),
        P(("groups", "orb")),
        P(("groups", "orb"), None),
    )
    out_specs = (P(("groups", "orb")), P(("groups", "orb"), None, None))
    return jax.shard_map(
        per_device, mesh=mesh, in_specs=in_specs, out_specs=out_specs, check_vma=False
    )
```

```python
import functools
import math

import jax
import jax.numpy as jnp
from jax import lax
from jax.experimental import pallas as pl
from jax.experimental.pallas import tpu as pltpu
from jax.sharding import PartitionSpec as P

GRAIN = 128
MESH = pl.DeviceIdType.MESH
NT = (((1,), (1,)), ((), ()))
TN = (((0,), (0,)), ((), ()))


def kernel(
    size, factor,
    blocks, pao_hbm, occ_hbm, dom_hbm, pairs_hbm,
    part, ret_in, energies,
    pao, occ, dom, pairs,
    own, got, left_t, info, linfo, wtab, wright, own_col, left_col, acc, ret_out, etab, ein, dens,
    small_sem, own_sem, blk_send, blk_recv, info_sem, w_sem, ret_send, ret_recv, e_sem, part_sem,
):
    n, _, width = blocks.shape
    tiles = width // GRAIN
    reach = n // 2
    edge = wright.shape[0]
    at_left, at_self = edge, 2 * edge
    me = lax.axis_index("orb")
    has_left = me > 0
    has_right = me < size - 1
    right = jnp.minimum(me + 1, size - 1)
    left = jnp.maximum(me - 1, 0)

    barrier = pltpu.get_barrier_semaphore()

    @pl.when(has_left)
    def _():
        pl.semaphore_signal(barrier, inc=1, device_id={"orb": left}, device_id_type=MESH)

    @pl.when(has_right)
    def _():
        pl.semaphore_signal(barrier, inc=1, device_id={"orb": right}, device_id_type=MESH)

    def own_copy(k):
        return pltpu.make_async_copy(blocks.at[k], own.at[k], own_sem.at[k])

    def to_right(source, target, send_sem, recv_sem):
        return pltpu.make_async_remote_copy(
            src_ref=source, dst_ref=target, send_sem=send_sem, recv_sem=recv_sem,
            device_id={"orb": right}, device_id_type=MESH,
        )

    def to_left(source, target, send_sem, recv_sem):
        return pltpu.make_async_remote_copy(
            src_ref=source, dst_ref=target, send_sem=send_sem, recv_sem=recv_sem,
            device_id={"orb": left}, device_id_type=MESH,
        )

    def blk_copy(k):
        return to_right(blocks.at[k], got.at[k], blk_send.at[k], blk_recv.at[k])

    def info_copy():
        return to_right(info, linfo, info_sem.at[0], info_sem.at[1])

    def w_copy():
        return to_right(wtab.at[pl.ds(0, edge)], wright, w_sem.at[0], w_sem.at[1])

    def ret_copy(k):
        return to_left(ret_out.at[k], ret_in.at[k], ret_send.at[k], ret_recv.at[k])

    def e_copy():
        return to_left(etab.at[pl.ds(at_left, edge)], ein, e_sem.at[0], e_sem.at[1])

    small = [
        pltpu.make_async_copy(source, target, small_sem.at[at])
        for at, (source, target) in enumerate(
            ((pao_hbm, pao), (occ_hbm, occ), (dom_hbm, dom), (pairs_hbm, pairs))
        )
    ]
    for copy in small:
        copy.start()
    peers = has_left.astype(jnp.int32) + has_right.astype(jnp.int32)
    pl.semaphore_wait(barrier, peers)

    @pl.when(has_right)
    def _():
        blk_copy(0).start()

    for k in range(n):
        own_copy(k).start()
    for copy in small:
        copy.wait()

    info[...] = jnp.zeros_like(info)
    column = lax.broadcasted_iota(jnp.int32, (1, width), 1)
    for k in range(n):
        info[k : k + 1, :] = pao[k : k + 1, :] - occ[k]
        info[8 + k : 9 + k, :] = jnp.where(column < dom[k] * GRAIN, 1.0, 0.0)

    start = me * n
    live = pairs[0:1, :] >= 0
    i = pairs[0:1, :] - start
    j = pairs[1:2, :] - start
    ahead = jnp.where(j < i, j - i + n, j - i)
    near = (ahead < n - ahead) | ((2 * ahead == n) & (i < j))
    place = at_self + jnp.where(near, i * reach + ahead - 1, j * reach + (n - ahead) - 1)
    place = jnp.where(j < 0, at_left + (j + n) * n + i, place)
    place = jnp.where(j >= n, i * n + (j - n), place)
    place = jnp.where(live, place, -1)
    spots = lax.broadcasted_iota(jnp.int32, (GRAIN, pairs.shape[1]), 0)
    hot = jnp.where(place == spots, 1.0, 0.0)
    counts = jnp.sum(hot, axis=1, keepdims=True)
    wtab[...] = jnp.broadcast_to(counts, (GRAIN, GRAIN))

    @pl.when(has_right)
    def _():
        info_copy().start()
        w_copy().start()
        for k in range(1, n):
            blk_copy(k).start()

    def columns(source, target):
        turned = jnp.transpose(source[0:8, :])
        for k in range(n):
            target[k] = jnp.broadcast_to(turned[:, k : k + 1], (width, GRAIN))

    def wide(x):
        return jnp.concatenate([x] * tiles, axis=1)

    columns(info, own_col)
    dens[...] = jnp.zeros_like(dens)
    etab[...] = jnp.zeros_like(etab)

    @pl.loop(0, n)
    def _(k):
        own_copy(k).wait()
        own[k] = own[k] * info[pl.ds(8 + k, 1), :].astype(jnp.bfloat16)

    def product(col, r, w, spot):
        exchange = jnp.dot(left_t[...], own[r], preferred_element_type=jnp.float32)
        denom = wide(col) + info[pl.ds(r, 1), :]
        amplitude = -exchange / denom
        parts = jnp.sum((exchange * amplitude).reshape(width // 8, 8, width), axis=0)
        energy = parts[:, :GRAIN]
        for c in range(1, tiles):
            energy = energy + parts[:, c * GRAIN : (c + 1) * GRAIN]
        etab[pl.ds(spot, 1), :] = jnp.sum(energy, axis=0, keepdims=True)
        rounded = amplitude.astype(jnp.bfloat16)
        first = lax.dot_general(rounded, rounded, NT, preferred_element_type=jnp.float32)
        second = lax.dot_general(rounded, rounded, TN, preferred_element_type=jnp.float32)
        scale = wide(w) * factor
        dens[r] += second * scale
        return first * scale

    @pl.loop(0, n)
    def _(i):
        left_t[...] = jnp.transpose(own[i])
        total = None
        for t in range(1, reach + 1):
            spot = at_self + i * reach + (t - 1)
            first = product(own_col[i], lax.rem(i + t, n), wtab[pl.ds(spot, 1), :], spot)
            total = first if total is None else total + first
        dens[i] += total

    upper = [(a, b) for a in range(tiles) for b in range(a, tiles)]
    step = 2 if n % 2 == 0 else 1

    @pl.when(has_left)
    def _():
        info_copy().wait_recv()
        w_copy().wait_recv()
        columns(linfo, left_col)

        @pl.loop(0, n)
        def _(k):
            blk_copy(k).wait_recv()

            @pl.when(k == n - 1)
            def _():
                @pl.loop(0, n - 1)
                def _(m):
                    ret_copy(m).start()

            left_t[...] = jnp.transpose(got[k] * linfo[pl.ds(8 + k, 1), :].astype(jnp.bfloat16))
            acc[...] = jnp.zeros_like(acc)

            @pl.loop(0, n // step)
            def _(q):
                total = None
                for s in range(step):
                    r = q * step + s
                    at = k * n + r
                    w = wright[pl.ds(at, 1), :] + wtab[pl.ds(at_left + at, 1), :]
                    first = product(left_col[k], r, w, at_left + at)
                    total = first if total is None else total + first
                acc[...] += total

            for u, (a, b) in enumerate(upper):
                ret_out[k, u] = acc[a * GRAIN : (a + 1) * GRAIN, b * GRAIN : (b + 1) * GRAIN].astype(jnp.bfloat16)

        e_copy().start()
        ret_copy(n - 1).start()

    def part_copy(k):
        return pltpu.make_async_copy(dens.at[k], part.at[k], part_sem.at[k])

    for k in range(n):
        part_copy(k).start()

    @pl.when(has_right)
    def _():
        info_copy().wait_send()
        w_copy().wait_send()

        @pl.loop(0, n)
        def _(k):
            blk_copy(k).wait_send()

        e_copy().wait_recv()
        etab[0:edge, :] = ein[...]

    table = jnp.sum(etab[...], axis=1, keepdims=True)
    energies[...] = 2.0 * jnp.sum(hot * table, axis=0, keepdims=True)

    for k in range(n):
        part_copy(k).wait()

    @pl.when(has_left)
    def _():
        e_copy().wait_send()

        @pl.loop(0, n)
        def _(k):
            ret_copy(k).wait_send()

    @pl.when(has_right)
    def _():
        @pl.loop(0, n)
        def _(k):
            ret_copy(k).wait_recv()


def add_returned(size, part, ret, out):
    tiles = part.shape[1] // GRAIN
    upper = [(a, b) for a in range(tiles) for b in range(a, tiles)]
    has_right = lax.axis_index("orb") < size - 1

    @pl.when(has_right)
    def _():
        for k in range(part.shape[0]):
            for u, (a, b) in enumerate(upper):
                rows, cols = pl.ds(a * GRAIN, GRAIN), pl.ds(b * GRAIN, GRAIN)
                term = ret[k, u].astype(jnp.float32)
                out[k, rows, cols] = part[k, rows, cols] + term
                if a != b:
                    out[k, cols, rows] = part[k, cols, rows] + jnp.transpose(term)

    @pl.when(jnp.logical_not(has_right))
    def _():
        out[...] = part[...]


def per_device(blocks, pao_energy, occ_energy, dom_blocks, pairs):
    n, aux, width = blocks.shape
    size = lax.axis_size("orb")
    factor = 1.0 / math.sqrt(width)
    edge = -(-n * n // 8) * 8
    tiles = width // GRAIN
    upper = tiles * (tiles + 1) // 2
    f32, bf16 = jnp.float32, jnp.bfloat16
    vmem = pl.BlockSpec(memory_space=pltpu.VMEM)
    hbm = pl.BlockSpec(memory_space=pl.ANY)
    many = pltpu.SemaphoreType.DMA((n,))
    two = pltpu.SemaphoreType.DMA((2,))
    slots = pairs.shape[0]
    part, ret, energies = pl.pallas_call(
        functools.partial(kernel, size, factor),
        out_shape=(
            jax.ShapeDtypeStruct((n, width, width), f32),
            jax.ShapeDtypeStruct((n, upper, GRAIN, GRAIN), bf16),
            jax.ShapeDtypeStruct((1, slots), f32),
        ),
        in_specs=[hbm] * 5,
        out_specs=(hbm, hbm, vmem),
        scratch_shapes=[
            pltpu.VMEM((n, width), f32),
            pltpu.SMEM((n,), f32),
            pltpu.SMEM((n,), jnp.int32),
            pltpu.VMEM((2, slots), jnp.int32),
            pltpu.VMEM((n, aux, width), bf16),
            pltpu.VMEM((n, aux, width), bf16),
            pltpu.VMEM((width, aux), bf16),
            pltpu.VMEM((16, width), f32),
            pltpu.VMEM((16, width), f32),
            pltpu.VMEM((GRAIN, GRAIN), f32),
            pltpu.VMEM((edge, GRAIN), f32),
            pltpu.VMEM((n, width, GRAIN), f32),
            pltpu.VMEM((n, width, GRAIN), f32),
            pltpu.VMEM((width, width), f32),
            pltpu.VMEM((n, upper, GRAIN, GRAIN), bf16),
            pltpu.VMEM((GRAIN, GRAIN), f32),
            pltpu.VMEM((edge, GRAIN), f32),
            pltpu.VMEM((n, width, width), f32),
            pltpu.SemaphoreType.DMA((4,)),
            many, many, many, two, two, many, many, two, many,
        ],
        compiler_params=pltpu.CompilerParams(
            collective_id=0, has_side_effects=True, vmem_limit_bytes=60 * 1024 * 1024
        ),
    )(blocks, pao_energy, occ_energy, dom_blocks, pairs.T)
    each = 2 if n % 2 == 0 else 1
    square = pl.BlockSpec((each, width, width), lambda k: (k, 0, 0))
    dens = pl.pallas_call(
        functools.partial(add_returned, size),
        grid=(n // each,),
        out_shape=jax.ShapeDtypeStruct((n, width, width), f32),
        in_specs=[square, pl.BlockSpec((each, upper, GRAIN, GRAIN), lambda k: (k, 0, 0, 0))],
        out_specs=square,
        compiler_params=pltpu.CompilerParams(vmem_limit_bytes=60 * 1024 * 1024),
    )(part, ret)
    return (energies.reshape(slots), dens)


def solution(mesh):
    in_specs = (
        P(("groups", "orb"), None, None),
        P(("groups", "orb"), None),
        P(("groups", "orb")),
        P(("groups", "orb")),
        P(("groups", "orb"), None),
    )
    out_specs = (P(("groups", "orb")), P(("groups", "orb"), None, None))
    return jax.shard_map(
        per_device, mesh=mesh, in_specs=in_specs, out_specs=out_specs, check_vma=False
    )
```

```python
import functools
import math

import jax
import jax.numpy as jnp
from jax import lax
from jax.experimental import pallas as pl
from jax.experimental.pallas import tpu as pltpu
from jax.sharding import PartitionSpec as P

GRAIN = 128
MESH = pl.DeviceIdType.MESH
NT = (((1,), (1,)), ((), ()))
TN = (((0,), (0,)), ((), ()))


def kernel(
    size, factor,
    blocks, pao_hbm, occ_hbm, dom_hbm, pairs_hbm,
    part, ret_in, energies,
    pao, occ, dom, pairs,
    own, got, left_t, info, linfo, wtab, wright, own_col, left_col, acc, ret_out, etab, ein, dens,
    small_sem, own_sem, blk_send, blk_recv, info_sem, w_sem, ret_send, ret_recv, e_sem, part_sem,
):
    n, _, width = blocks.shape
    tiles = width // GRAIN
    reach = n // 2
    edge = wright.shape[0]
    at_left, at_self = edge, 2 * edge
    me = lax.axis_index("orb")
    has_left = me > 0
    has_right = me < size - 1
    right = jnp.minimum(me + 1, size - 1)
    left = jnp.maximum(me - 1, 0)

    barrier = pltpu.get_barrier_semaphore()

    @pl.when(has_left)
    def _():
        pl.semaphore_signal(barrier, inc=1, device_id={"orb": left}, device_id_type=MESH)

    @pl.when(has_right)
    def _():
        pl.semaphore_signal(barrier, inc=1, device_id={"orb": right}, device_id_type=MESH)

    def own_copy(k):
        return pltpu.make_async_copy(blocks.at[k], own.at[k], own_sem.at[k])

    def to_right(source, target, send_sem, recv_sem):
        return pltpu.make_async_remote_copy(
            src_ref=source, dst_ref=target, send_sem=send_sem, recv_sem=recv_sem,
            device_id={"orb": right}, device_id_type=MESH,
        )

    def to_left(source, target, send_sem, recv_sem):
        return pltpu.make_async_remote_copy(
            src_ref=source, dst_ref=target, send_sem=send_sem, recv_sem=recv_sem,
            device_id={"orb": left}, device_id_type=MESH,
        )

    def blk_copy(k):
        return to_right(blocks.at[k], got.at[k], blk_send.at[k], blk_recv.at[k])

    def info_copy():
        return to_right(info, linfo, info_sem.at[0], info_sem.at[1])

    def w_copy():
        return to_right(wtab.at[pl.ds(0, edge)], wright, w_sem.at[0], w_sem.at[1])

    def ret_copy(k):
        return to_left(ret_out.at[k], ret_in.at[k], ret_send.at[k], ret_recv.at[k])

    def e_copy():
        return to_left(etab.at[pl.ds(at_left, edge)], ein, e_sem.at[0], e_sem.at[1])

    small = [
        pltpu.make_async_copy(source, target, small_sem.at[at])
        for at, (source, target) in enumerate(
            ((pao_hbm, pao), (occ_hbm, occ), (dom_hbm, dom), (pairs_hbm, pairs))
        )
    ]
    for copy in small:
        copy.start()
    peers = has_left.astype(jnp.int32) + has_right.astype(jnp.int32)
    pl.semaphore_wait(barrier, peers)

    @pl.when(has_right)
    def _():
        blk_copy(0).start()

    for k in range(n):
        own_copy(k).start()
    for copy in small:
        copy.wait()

    info[...] = jnp.zeros_like(info)
    column = lax.broadcasted_iota(jnp.int32, (1, width), 1)
    for k in range(n):
        info[k : k + 1, :] = pao[k : k + 1, :] - occ[k]
        info[8 + k : 9 + k, :] = jnp.where(column < dom[k] * GRAIN, 1.0, 0.0)

    start = me * n
    live = pairs[0:1, :] >= 0
    i = pairs[0:1, :] - start
    j = pairs[1:2, :] - start
    ahead = jnp.where(j < i, j - i + n, j - i)
    near = (ahead < n - ahead) | ((2 * ahead == n) & (i < j))
    place = at_self + jnp.where(near, i * reach + ahead - 1, j * reach + (n - ahead) - 1)
    place = jnp.where(j < 0, at_left + (j + n) * n + i, place)
    place = jnp.where(j >= n, i * n + (j - n), place)
    place = jnp.where(live, place, -1)
    spots = lax.broadcasted_iota(jnp.int32, (GRAIN, pairs.shape[1]), 0)
    hot = jnp.where(place == spots, 1.0, 0.0)
    counts = jnp.sum(hot, axis=1, keepdims=True)
    wtab[...] = jnp.broadcast_to(counts, (GRAIN, GRAIN))

    @pl.when(has_right)
    def _():
        info_copy().start()
        w_copy().start()
        for k in range(1, n):
            blk_copy(k).start()

    def columns(source, target):
        turned = jnp.transpose(source[0:8, :])
        for k in range(n):
            target[k] = jnp.broadcast_to(turned[:, k : k + 1], (width, GRAIN))

    def wide(x):
        return jnp.concatenate([x] * tiles, axis=1)

    columns(info, own_col)
    dens[...] = jnp.zeros_like(dens)
    etab[...] = jnp.zeros_like(etab)

    @pl.loop(0, n)
    def _(k):
        own_copy(k).wait()
        own[k] = own[k] * info[pl.ds(8 + k, 1), :].astype(jnp.bfloat16)

    def product(col, r, w, spot):
        exchange = jnp.dot(left_t[...], own[r], preferred_element_type=jnp.float32)
        denom = wide(col) + info[pl.ds(r, 1), :]
        amplitude = -exchange / denom
        parts = jnp.sum((exchange * amplitude).reshape(width // 8, 8, width), axis=0)
        energy = parts[:, :GRAIN]
        for c in range(1, tiles):
            energy = energy + parts[:, c * GRAIN : (c + 1) * GRAIN]
        etab[pl.ds(spot, 1), :] = jnp.sum(energy, axis=0, keepdims=True)
        rounded = amplitude.astype(jnp.bfloat16)
        first = lax.dot_general(rounded, rounded, NT, preferred_element_type=jnp.float32)
        second = lax.dot_general(rounded, rounded, TN, preferred_element_type=jnp.float32)
        scale = wide(w) * factor
        dens[r] += second * scale
        return first * scale

    @pl.loop(0, n)
    def _(i):
        left_t[...] = jnp.transpose(own[i])
        total = None
        for t in range(1, reach + 1):
            spot = at_self + i * reach + (t - 1)
            first = product(own_col[i], lax.rem(i + t, n), wtab[pl.ds(spot, 1), :], spot)
            total = first if total is None else total + first
        dens[i] += total

    upper = [(a, b) for a in range(tiles) for b in range(a, tiles)]
    step = 2 if n % 2 == 0 else 1

    @pl.when(has_left)
    def _():
        info_copy().wait_recv()
        w_copy().wait_recv()
        columns(linfo, left_col)

        @pl.loop(0, n)
        def _(k):
            blk_copy(k).wait_recv()

            @pl.when(k == n - 1)
            def _():
                @pl.loop(0, n - 1)
                def _(m):
                    ret_copy(m).start()

            left_t[...] = jnp.transpose(got[k] * linfo[pl.ds(8 + k, 1), :].astype(jnp.bfloat16))
            acc[...] = jnp.zeros_like(acc)

            @pl.loop(0, n // step)
            def _(q):
                total = None
                for s in range(step):
                    r = q * step + s
                    at = k * n + r
                    w = wright[pl.ds(at, 1), :] + wtab[pl.ds(at_left + at, 1), :]
                    first = product(left_col[k], r, w, at_left + at)
                    total = first if total is None else total + first
                acc[...] += total

            for u, (a, b) in enumerate(upper):
                ret_out[k, u] = acc[a * GRAIN : (a + 1) * GRAIN, b * GRAIN : (b + 1) * GRAIN].astype(jnp.bfloat16)

        e_copy().start()
        ret_copy(n - 1).start()

    def part_copy(k):
        return pltpu.make_async_copy(dens.at[k], part.at[k], part_sem.at[k])

    for k in range(n):
        part_copy(k).start()

    @pl.when(has_right)
    def _():
        info_copy().wait_send()
        w_copy().wait_send()

        @pl.loop(0, n)
        def _(k):
            blk_copy(k).wait_send()

        e_copy().wait_recv()
        etab[0:edge, :] = ein[...]

    table = jnp.sum(etab[...], axis=1, keepdims=True)
    energies[...] = 2.0 * jnp.sum(hot * table, axis=0, keepdims=True)

    for k in range(n):
        part_copy(k).wait()

    @pl.when(has_left)
    def _():
        e_copy().wait_send()

        @pl.loop(0, n)
        def _(k):
            ret_copy(k).wait_send()

    @pl.when(has_right)
    def _():
        @pl.loop(0, n)
        def _(k):
            ret_copy(k).wait_recv()


def add_returned(size, part, ret, out):
    tiles = part.shape[1] // GRAIN
    upper = [(a, b) for a in range(tiles) for b in range(a, tiles)]
    has_right = lax.axis_index("orb") < size - 1

    @pl.when(has_right)
    def _():
        for k in range(part.shape[0]):
            for u, (a, b) in enumerate(upper):
                rows, cols = pl.ds(a * GRAIN, GRAIN), pl.ds(b * GRAIN, GRAIN)
                term = ret[k, u].astype(jnp.float32)
                out[k, rows, cols] = part[k, rows, cols] + term
                if a != b:
                    out[k, cols, rows] = part[k, cols, rows] + jnp.transpose(term)

    @pl.when(jnp.logical_not(has_right))
    def _():
        out[...] = part[...]


def per_device(blocks, pao_energy, occ_energy, dom_blocks, pairs):
    n, aux, width = blocks.shape
    size = lax.axis_size("orb")
    factor = 1.0 / math.sqrt(width)
    edge = -(-n * n // 8) * 8
    tiles = width // GRAIN
    upper = tiles * (tiles + 1) // 2
    f32, bf16 = jnp.float32, jnp.bfloat16
    vmem = pl.BlockSpec(memory_space=pltpu.VMEM)
    hbm = pl.BlockSpec(memory_space=pl.ANY)
    many = pltpu.SemaphoreType.DMA((n,))
    two = pltpu.SemaphoreType.DMA((2,))
    slots = pairs.shape[0]
    part, ret, energies = pl.pallas_call(
        functools.partial(kernel, size, factor),
        out_shape=(
            jax.ShapeDtypeStruct((n, width, width), f32),
            jax.ShapeDtypeStruct((n, upper, GRAIN, GRAIN), bf16),
            jax.ShapeDtypeStruct((1, slots), f32),
        ),
        in_specs=[hbm] * 5,
        out_specs=(hbm, hbm, vmem),
        scratch_shapes=[
            pltpu.VMEM((n, width), f32),
            pltpu.SMEM((n,), f32),
            pltpu.SMEM((n,), jnp.int32),
            pltpu.VMEM((2, slots), jnp.int32),
            pltpu.VMEM((n, aux, width), bf16),
            pltpu.VMEM((n, aux, width), bf16),
            pltpu.VMEM((width, aux), bf16),
            pltpu.VMEM((16, width), f32),
            pltpu.VMEM((16, width), f32),
            pltpu.VMEM((GRAIN, GRAIN), f32),
            pltpu.VMEM((edge, GRAIN), f32),
            pltpu.VMEM((n, width, GRAIN), f32),
            pltpu.VMEM((n, width, GRAIN), f32),
            pltpu.VMEM((width, width), f32),
            pltpu.VMEM((n, upper, GRAIN, GRAIN), bf16),
            pltpu.VMEM((GRAIN, GRAIN), f32),
            pltpu.VMEM((edge, GRAIN), f32),
            pltpu.VMEM((n, width, width), f32),
            pltpu.SemaphoreType.DMA((4,)),
            many, many, many, two, two, many, many, two, many,
        ],
        compiler_params=pltpu.CompilerParams(
            collective_id=0, has_side_effects=True, vmem_limit_bytes=60 * 1024 * 1024
        ),
    )(blocks, pao_energy, occ_energy, dom_blocks, pairs.T)
    each = 3 if n % 3 == 0 else 1
    square = pl.BlockSpec((each, width, width), lambda k: (k, 0, 0))
    dens = pl.pallas_call(
        functools.partial(add_returned, size),
        grid=(n // each,),
        out_shape=jax.ShapeDtypeStruct((n, width, width), f32),
        in_specs=[square, pl.BlockSpec((each, upper, GRAIN, GRAIN), lambda k: (k, 0, 0, 0))],
        out_specs=square,
        compiler_params=pltpu.CompilerParams(vmem_limit_bytes=60 * 1024 * 1024),
    )(part, ret)
    return (energies.reshape(slots), dens)


def solution(mesh):
    in_specs = (
        P(("groups", "orb"), None, None),
        P(("groups", "orb"), None),
        P(("groups", "orb")),
        P(("groups", "orb")),
        P(("groups", "orb"), None),
    )
    out_specs = (P(("groups", "orb")), P(("groups", "orb"), None, None))
    return jax.shard_map(
        per_device, mesh=mesh, in_specs=in_specs, out_specs=out_specs, check_vma=False
    )
```
